32 devices in a mesh: dp: 4 (over z), section: 4 (over y, x), expert: 2 (over core).
Axes of the slice: x: 2, y: 2, z: 4, core: 2. Of those that a mesh axis runs over, the one named last changes fastest.
Arguments:
- tokens: bfloat16 [1024, 5120], P(('dp', 'expert')), may hold values from -6 to 6
- cotangent: bfloat16 [1024, 5120], P(('dp', 'expert')), may hold values from -6 to 6
- norm_gain: float32 [4, 5120], P('section'), may hold values from 0.25 to 1.75
- route_gates: float32 [4, 1024, 6], P('section', ('dp', 'expert')), may hold values from 0.5 to 2
- expert_ids: int32 [4, 1024, 6], P('section', ('dp', 'expert')), may hold values from 0 to 159, as said below
- expert_map: int32 [4, 2], P('section'), may hold values from 0 to 1, each once within a row
- w_gate: bfloat16 [4, 2, 5120, 768], P('section', 'expert', 'dp'), may hold values from -0.078125 to 0.078125
- w_up: bfloat16 [4, 2, 5120, 768], P('section', 'expert', 'dp'), may hold values from -0.078125 to 0.078125
- w_down: bfloat16 [4, 2, 768, 5120], P('section', 'expert', None, 'dp'), may hold values from -0.21875 to 0.21875
Outputs:
- layer_out: bfloat16 [4, 1024, 5120], P('section', ('dp', 'expert'))
- input_grad: bfloat16 [4, 1024, 5120], P('section', ('dp', 'expert'))
- grad_gate: bfloat16 [4, 2, 5120, 768], P('section', 'expert', 'dp')
- grad_up: bfloat16 [4, 2, 5120, 768], P('section', 'expert', 'dp')
- grad_down: bfloat16 [4, 2, 768, 5120], P('section', 'expert', None, 'dp')
The draws below stay inside these ranges and needn't reach their ends.
Inputs may be any that keep to these rules, and one draw needn't show every extreme that they name: `expert_ids`: each token names 6 different experts on each layer. The held experts are those below 2. Split the 128 tokens of one index pair of dp and expert in order into 4 equal blocks: in each block each held expert is named by at most 2 tokens, and on every layer one held expert is named by exactly 2 tokens of every block, so by 8 tokens of every such pair. `expert_map`: each layer's row names every held expert once.
All inputs are finite; a program needn't handle non-finite values.
Results may differ from the reference program's by a relative error of at most 0.03.
Values may be sent and summed in bfloat16 or wider, within the bound.
A program may use at most 128 MiB of HBM per device.

```python
import jax
import jax.numpy as jnp
from jax import lax

D = 5120
H = 768
NEXP = 160
TOPK = 6
MICRO = 4
CAP_MB = 2
TOK_DEV = 128
CAP = 8
SECTIONS = 4
E_WIN = 2
TOKENS = 1024
N_DP = 4
N_EXPERT = 2


def draw_expert_ids(key, part):
    span = TOK_DEV // MICRO
    blocks = TOKENS // span
    keys = jax.random.split(jax.random.fold_in(key, 11), 4)
    base = jax.random.randint(keys[0], (SECTIONS, TOKENS, NEXP), 0, 2 ** 20) * NEXP + jnp.arange(NEXP, dtype=jnp.int32)
    counts = jax.random.randint(keys[1], (SECTIONS, blocks, E_WIN), (CAP_MB + 1) // 2, CAP_MB + 1)
    fullest = jax.random.randint(keys[2], (SECTIONS, 1, 1), 0, E_WIN)
    column = jnp.arange(E_WIN, dtype=jnp.int32)
    is_full = column[None, None, :] == fullest
    counts = jnp.where(is_full, CAP_MB, counts)
    noise = jax.random.randint(keys[3], (SECTIONS, blocks, E_WIN, span), 0, 2 ** 20) * span + jnp.arange(span, dtype=jnp.int32)
    ranks = jnp.argsort(jnp.argsort(noise, axis=-1), axis=-1)
    chosen = ranks < counts[..., None]
    chosen = jnp.transpose(chosen, (0, 1, 3, 2)).reshape(SECTIONS, TOKENS, E_WIN)
    held_scores = jnp.where(chosen, jnp.where(is_full, 2 ** 29, 2 ** 28 + column[None, None, :]), -1 - column[None, None, :])
    scores = jnp.concatenate([held_scores.astype(jnp.int32), base[:, :, E_WIN:].astype(jnp.int32)], axis=2)
    return lax.top_k(scores, TOPK)[1].astype(jnp.int32)


def levels(key, extent, shards, smallest, high):
    loudness, own = 1.0, jax.random.fold_in(key, 6)
    for position, parts in shards:
        steps = jnp.exp(jax.random.uniform(jax.random.fold_in(own, position), (parts,), jnp.float32, smallest / len(shards), high / len(shards)))
        loudness = loudness * jnp.repeat(steps, extent[position] // parts).reshape([-1 if axis == position else 1 for axis in range(len(extent))])
    return loudness


def centred(stream_key, extent, scale, bound, cuts=(), held_as=jnp.bfloat16):
    entries = scale * jax.random.normal(stream_key, extent, jnp.float32)
    if cuts:
        entries = entries * levels(stream_key, extent, cuts, -0.22, 0.18)
    return jnp.clip(entries, -bound, bound).astype(held_as)


def setup_inputs(seed: int = 0) -> dict:
    streams_of = jax.random.split(jax.random.key(seed), 10)
    tokens = centred(streams_of[0], (TOKENS, D), 1.0, 6.0, ((0, 8),))
    cotangent = centred(streams_of[1], (TOKENS, D), 1.0, 6.0, ((0, 8),))
    norm_gain = jnp.clip(1.0 + 0.15 * jax.random.normal(streams_of[2], (SECTIONS, D), jnp.float32), 0.25, 1.75)
    route_gates = jnp.clip(0.5 + 1.5 * jax.random.uniform(streams_of[3], (SECTIONS, TOKENS, TOPK), jnp.float32) ** levels(streams_of[3], (SECTIONS, TOKENS, TOPK), ((0, 4), (1, 8)), -0.2, 0.2), 0.5, 2.0)
    expert_ids = draw_expert_ids(jax.random.fold_in(streams_of[9], 71), 0)
    expert_map = jax.vmap(lambda own: jax.random.permutation(own, E_WIN))(jax.random.split(streams_of[5], SECTIONS)).reshape((SECTIONS, E_WIN)).astype(jnp.int32)
    w_gate = centred(streams_of[6], (SECTIONS, E_WIN, D, H), D ** -0.5, 0.078125, ((0, 4), (1, 2), (2, 4)))
    w_up = centred(streams_of[7], (SECTIONS, E_WIN, D, H), D ** -0.5, 0.078125, ((0, 4), (1, 2), (2, 4)))
    w_down = centred(streams_of[8], (SECTIONS, E_WIN, H, D), H ** -0.5, 0.21875, ((0, 4), (1, 2), (3, 4)))
    return {"tokens": tokens, "cotangent": cotangent, "norm_gain": norm_gain, "route_gates": route_gates, "expert_ids": expert_ids, "expert_map": expert_map, "w_gate": w_gate, "w_up": w_up, "w_down": w_down}


def reference(tokens, cotangent, norm_gain, route_gates, expert_ids, expert_map, w_gate, w_up, w_down):
    slot_total = N_DP * N_EXPERT * CAP
    current = tokens
    outputs = []
    records = []
    for layer in range(SECTIONS):
        wide_in = current.astype(jnp.float32)
        inv_rms = lax.rsqrt(lax.optimization_barrier(jnp.mean(wide_in * wide_in, axis=1, keepdims=True)) + 1e-06)
        normed = (wide_in * inv_rms * norm_gain[layer][None, :]).astype(jnp.bfloat16)
        combined = jnp.zeros((TOKENS, D), jnp.float32)
        details = []
        for column in range(E_WIN):
            expert = expert_map[layer, column]
            matches = expert_ids[layer] == expert
            chosen = jnp.any(matches, axis=1)
            weight_row = lax.optimization_barrier(jnp.sum(jnp.where(matches, route_gates[layer], jnp.float32(0.0)), axis=1))
            picked = jnp.nonzero(chosen, size=slot_total, fill_value=TOKENS)[0].astype(jnp.int32)
            slot_rows = jnp.take(normed, picked, axis=0, mode='fill', fill_value=0)
            slot_weight = jnp.take(weight_row, picked, axis=0, mode='fill', fill_value=0)
            gate_pre = jnp.dot(slot_rows, w_gate[layer, column], preferred_element_type=jnp.float32)
            up_pre = jnp.dot(slot_rows, w_up[layer, column], preferred_element_type=jnp.float32)
            activated = (gate_pre * jax.nn.sigmoid(gate_pre) * up_pre).astype(jnp.bfloat16)
            expert_out = jnp.dot(activated, w_down[layer, column], preferred_element_type=jnp.float32).astype(jnp.bfloat16)
            combined = combined.at[picked].add(slot_weight[:, None] * expert_out.astype(jnp.float32), mode='drop')
            details.append((picked, slot_rows, slot_weight, gate_pre, up_pre, activated))
        result = (wide_in + combined).astype(jnp.bfloat16)
        outputs.append(result)
        records.append((wide_in, inv_rms, details))
        current = result
    incoming = cotangent
    input_grads = [None] * SECTIONS
    gate_grads = [None] * SECTIONS
    up_grads = [None] * SECTIONS
    down_grads = [None] * SECTIONS
    for layer in range(SECTIONS - 1, -1, -1):
        wide_in, inv_rms, details = records[layer]
        grad_wide = incoming.astype(jnp.float32)
        normed_grad = jnp.zeros((TOKENS, D), jnp.float32)
        layer_gate = []
        layer_up = []
        layer_down = []
        for column in range(E_WIN):
            picked, slot_rows, slot_weight, gate_pre, up_pre, activated = details[column]
            slot_grad = (slot_weight[:, None] * jnp.take(grad_wide, picked, axis=0, mode='fill', fill_value=0)).astype(jnp.bfloat16)
            layer_down.append(jnp.dot(activated.T, slot_grad, preferred_element_type=jnp.float32).astype(jnp.bfloat16))
            hidden_grad = jnp.dot(slot_grad, w_down[layer, column].T, preferred_element_type=jnp.float32)
            sigma = jax.nn.sigmoid(gate_pre)
            gate_grad = (hidden_grad * up_pre * sigma * (1.0 + gate_pre * (1.0 - sigma))).astype(jnp.bfloat16)
            up_grad = (hidden_grad * gate_pre * sigma).astype(jnp.bfloat16)
            layer_gate.append(jnp.dot(slot_rows.T, gate_grad, preferred_element_type=jnp.float32).astype(jnp.bfloat16))
            layer_up.append(jnp.dot(slot_rows.T, up_grad, preferred_element_type=jnp.float32).astype(jnp.bfloat16))
            slot_back = (jnp.dot(gate_grad, w_gate[layer, column].T, preferred_element_type=jnp.float32) + jnp.dot(up_grad, w_up[layer, column].T, preferred_element_type=jnp.float32)).astype(jnp.bfloat16)
            normed_grad = normed_grad.at[picked].add(slot_back.astype(jnp.float32), mode='drop')
        scaled_grad = normed_grad * norm_gain[layer][None, :]
        through_norm = inv_rms * (scaled_grad - wide_in * inv_rms * inv_rms * lax.optimization_barrier(jnp.mean(scaled_grad * wide_in, axis=1, keepdims=True)))
        incoming = (grad_wide + through_norm).astype(jnp.bfloat16)
        input_grads[layer] = incoming
        gate_grads[layer] = jnp.stack(layer_gate)
        up_grads[layer] = jnp.stack(layer_up)
        down_grads[layer] = jnp.stack(layer_down)
    return (jnp.stack(outputs), jnp.stack(input_grads), jnp.stack(gate_grads), jnp.stack(up_grads), jnp.stack(down_grads))
```

```python
import functools

import jax
import jax.numpy as jnp
from jax import lax
from jax.experimental import pallas as pl
from jax.experimental.pallas import tpu as pltpu
from jax.sharding import PartitionSpec as P

CAP = 8
EPS = 1e-06
F32 = jnp.float32
BF16 = jnp.bfloat16
FIRST = (((0,), (0,)), ((), ()))
SECOND = (((1,), (1,)), ((), ()))


def split(value):
    high = value.astype(BF16)
    return high, (value - high.astype(F32)).astype(BF16)


def join(ref_value):
    wide = ref_value.astype(F32)
    return wide[:, :128] + wide[:, 128:]


def kernel(
    nz, nl, ne,
    tok_in, cot_in, gain, gates, ids, emap, wg_in, wu_in, wd_in,
    out_f, out_b, out_g, out_u, out_d,
    tok, cot, wg, wu, wd,
    d_send, d_recv, m_send, m_recv, idsall, cross, own_b, r_send, r_recv,
    a_ref, g_ref, part, part_in, act_all, hpart, hpart_in, grad_all,
    gp_ref, up_ref, inv_ref,
    load_sem, store_sem, d_ss, d_rs, m_ss, m_rs, i_ss, i_rs, c_ss, c_rs,
    f_ss, f_rs, x_ss, x_rs, r_ss, r_rs,
):
    z, s, p = lax.axis_index("dp"), lax.axis_index("section"), lax.axis_index("expert")
    nb = nz * ne
    me = z * ne + p
    rows = ne * CAP
    slots = nb * CAP
    toks, width = tok.shape
    dsl = width // nz
    half = dsl // 2
    hid = wg.shape[1]

    def rdma(src, dst, ss, rs, zz, sec, ex):
        return pltpu.make_async_remote_copy(
            src_ref=src, dst_ref=dst, send_sem=ss, recv_sem=rs,
            device_id={"dp": zz, "section": sec, "expert": ex},
            device_id_type=pl.DeviceIdType.MESH,
        )

    loads = [
        pltpu.make_async_copy(a, b, load_sem.at[i])
        for i, (a, b) in enumerate(
            ((tok_in, tok), (cot_in, cot), (wg_in, wg), (wu_in, wu), (wd_in, wd))
        )
    ]
    for copy in loads:
        copy.start()

    barrier = pltpu.get_barrier_semaphore()

    def greet(d, _):
        other = lax.rem(me + d, nb)
        pl.semaphore_signal(
            barrier, inc=1,
            device_id={"dp": other // ne, "section": s, "expert": lax.rem(other, ne)},
            device_id_type=pl.DeviceIdType.MESH,
        )
        return 0

    lax.fori_loop(1, nb, greet, 0)

    def greet_section(d, _):
        pl.semaphore_signal(
            barrier, inc=1,
            device_id={"dp": z, "section": lax.rem(s + d, nl), "expert": p},
            device_id_type=pl.DeviceIdType.MESH,
        )
        return 0

    lax.fori_loop(1, nl, greet_section, 0)

    lane = lax.broadcasted_iota(jnp.int32, (toks, 128), 1)
    row = lax.broadcasted_iota(jnp.int32, (toks, 128), 0)
    expert = jnp.full((toks, 128), -1, jnp.int32)
    place = lane
    for e in range(ne):
        here = (lane >= e * CAP) & (lane < (e + 1) * CAP)
        expert = jnp.where(here, emap[0, e], expert)
        place = jnp.where(here, lane - e * CAP, place)
    chosen = jnp.zeros((toks, 128), F32)
    weight = jnp.zeros((toks, 128), F32)
    for k in range(ids.shape[1]):
        match = ids[:, k : k + 1] == expert
        chosen = chosen + jnp.where(match, 1.0, 0.0)
        weight = weight + jnp.where(match, gates[:, k : k + 1], 0.0)
    tri_r = lax.broadcasted_iota(jnp.int32, (toks, toks), 0)
    tri_c = lax.broadcasted_iota(jnp.int32, (toks, toks), 1)
    tri = jnp.where(tri_r >= tri_c, 1.0, 0.0).astype(BF16)
    rank = jnp.dot(tri, chosen.astype(BF16), preferred_element_type=F32)
    placed = jnp.where(rank - 1.0 == place.astype(F32), chosen, 0.0)
    placed_t = jnp.transpose(placed)[:rows]
    r_col = jnp.sum(jnp.transpose(placed * weight)[:rows], axis=1, keepdims=True)
    t_col = jnp.sum(
        jnp.transpose(placed * (row + 1).astype(F32))[:rows], axis=1, keepdims=True
    )
    base = (me * toks).astype(F32)
    t_col = jnp.where(t_col > 0.5, t_col - 1.0 + base, -1.0)
    m_send[:, :128] = jnp.broadcast_to(r_col, (rows, 128))
    m_send[:, 128:] = jnp.broadcast_to(t_col, (rows, 128))
    m_recv[me] = m_send[...]
    pick = placed_t.astype(BF16)

    pl.semaphore_wait(barrier, nb - 1 + nl - 1)

    def pack(value):
        return jnp.concatenate([value[..., :half], value[..., half:]], axis=-2)

    def gather(kind, source):
        for q in range(nz):
            got = jnp.dot(
                pick, source[:, q * dsl : (q + 1) * dsl], preferred_element_type=F32
            )
            for e in range(ne):
                d_send[kind, q * ne + e] = pack(got[e * CAP : (e + 1) * CAP]).astype(BF16)
        d_recv[kind, me] = d_send[kind, me]

    def dispatch(kind):
        def send(d, _):
            other = lax.rem(me + d, nb)
            rdma(
                d_send.at[kind, other], d_recv.at[kind, me], d_ss.at[kind, d], d_rs.at[kind, d],
                other // ne, s, lax.rem(other, ne),
            ).start()
            return 0

        lax.fori_loop(1, nb, send, 0)

    def dispatch_wait(kind, sent):
        def wait(d, _):
            other = lax.rem(me + nb - d, nb)
            copy = rdma(
                d_send.at[kind, other], d_recv.at[kind, other], d_ss.at[kind, d],
                d_rs.at[kind, d], other // ne, s, lax.rem(other, ne),
            )
            if sent:
                copy.wait_send()
            else:
                copy.wait_recv()
            return 0

        lax.fori_loop(1, nb, wait, 0)

    def meta(action):
        def step(d, _):
            other = lax.rem(me + d, nb)
            source = lax.rem(me + nb - d, nb)
            where = me if action == "start" else source
            copy = rdma(
                m_send, m_recv.at[where], m_ss.at[d], m_rs.at[d],
                other // ne, s, lax.rem(other, ne),
            )
            getattr(copy, action)()
            return 0

        lax.fori_loop(1, nb, step, 0)

    def exchange_ids(action):
        def step(d, _):
            other = lax.rem(s + d, nl)
            source = lax.rem(s + nl - d, nl)
            where = s if action == "start" else source
            copy = rdma(idsall.at[s], idsall.at[where], i_ss.at[d], i_rs.at[d], z, other, p)
            getattr(copy, action)()
            return 0

        lax.fori_loop(1, nl, step, 0)

    meta("start")
    loads[0].wait()
    gather(0, tok)
    dispatch(0)
    loads[1].wait()
    gather(1, cot)
    dispatch(1)
    meta("wait_recv")
    idsall[s] = m_recv[:, :, 128:]
    exchange_ids("start")

    own_rows = pl.ds(pl.multiple_of(p * CAP, CAP), CAP)
    own_meta = m_recv[:, own_rows, :].reshape(slots, 256)
    r_slot = own_meta[:, 0:1]
    t_slot = own_meta[:, 128:129]
    gain_row = gain[:, pl.ds(pl.multiple_of(z * dsl, 128), dsl)]

    def unpack(kind):
        value = d_recv[kind].astype(F32)
        return jnp.concatenate([value[:, :CAP], value[:, CAP:]], axis=-1).reshape(slots, dsl)

    dispatch_wait(0, False)
    a_ref[...] = unpack(0)

    def over_dp(action, send_at, recv_at, which):
        def step(d, _):
            other = lax.rem(z + d, nz)
            source = lax.rem(z + nz - d, nz)
            where = z if action == "start" else source
            copy = rdma(
                send_at(other), recv_at(where), c_ss.at[which, d], c_rs.at[which, d],
                other, s, p,
            )
            getattr(copy, action)()
            return 0

        lax.fori_loop(1, nz, step, 0)

    def block(ref):
        return lambda other: ref.at[pl.ds(pl.multiple_of(other * rows, 16), rows)]

    def mine(ref):
        return lambda other: ref.at[z]

    def at(ref):
        return lambda where: ref.at[where]

    def return_rows(kind, layer, value):
        r_send[kind, layer] = pack(value.reshape(nb, CAP, dsl)).astype(BF16)
        r_recv[kind, layer, me] = r_send[kind, layer, me]

        def send(d, _):
            other = lax.rem(me + d, nb)
            rdma(
                r_send.at[kind, layer, other], r_recv.at[kind, layer, me],
                r_ss.at[kind, layer, d], r_rs.at[kind, layer, d],
                other // ne, s, lax.rem(other, ne),
            ).start()
            return 0

        lax.fori_loop(1, nb, send, 0)

    def return_wait(kind, layer, sent):
        def wait(d, _):
            other = lax.rem(me + nb - d, nb)
            copy = rdma(
                r_send.at[kind, layer, other], r_recv.at[kind, layer, other],
                r_ss.at[kind, layer, d], r_rs.at[kind, layer, d],
                other // ne, s, lax.rem(other, ne),
            )
            if sent:
                copy.wait_send()
            else:
                copy.wait_recv()
            return 0

        lax.fori_loop(1, nb, wait, 0)

    def to_section(kind, layer, src, sec):
        return rdma(
            src, cross.at[layer, p], f_ss.at[kind, layer], f_rs.at[kind, layer], z, sec, p
        )

    def share(layer, action):
        def step(d, _):
            other = lax.rem(p + d, ne)
            source = lax.rem(p + ne - d, ne)
            where = p if action != "wait_recv" else source
            copy = rdma(
                cross.at[layer, p], cross.at[layer, where], x_ss.at[layer, d],
                x_rs.at[layer, d], z, s, other,
            )
            getattr(copy, action)()
            return 0

        lax.fori_loop(1, ne, step, 0)

    def receive(kind, layer, state, step_to, last):
        matches = []
        for e in range(ne):
            theirs = idsall[layer, :, e * CAP : (e + 1) * CAP, :].reshape(slots, 128)
            theirs = jnp.transpose(theirs)[0:1]
            matches.append(jnp.where(t_slot == theirs, 1.0, 0.0).astype(BF16))
        to_section(kind, layer, cross.at[layer, p], lax.rem(s + nl + step_to, nl)).wait_recv()
        share(layer, "start")

        @pl.when(s != last)
        def _():
            to_section(kind, layer, cross.at[layer, p], lax.rem(s + nl + step_to, nl)).start()

        share(layer, "wait_recv")
        total = state[...]
        for e in range(ne):
            total = total + jnp.dot(matches[e], cross[layer, e], preferred_element_type=F32)
        state[...] = total.astype(BF16).astype(F32)
        return_rows(kind, layer, cross[layer, p].astype(F32))

    exchange_ids("wait_recv")

    def forward_receive(layer, _):
        receive(0, layer, a_ref, 1, nl - 1)
        return 0

    lax.fori_loop(0, s, forward_receive, 0)

    wide = a_ref[...]
    x = (wide * gain_row).astype(BF16)
    square = jnp.sum(wide * wide, axis=1, keepdims=True)
    loads[2].wait()
    part[:, :hid] = jnp.dot(x, wg[...], preferred_element_type=F32).astype(BF16)
    loads[3].wait()
    part[:, hid : 2 * hid] = jnp.dot(x, wu[...], preferred_element_type=F32).astype(BF16)
    high, low = split(jnp.broadcast_to(square, (slots, 128)))
    part[:, 2 * hid : 2 * hid + 128] = high
    part[:, 2 * hid + 128 :] = low
    over_dp("start", block(part), at(part_in), 0)
    part_in[z] = part[pl.ds(pl.multiple_of(z * rows, 16), rows)]
    over_dp("wait_recv", block(part), at(part_in), 0)
    total = part_in[0].astype(F32)
    for i in range(1, nz):
        total = total + part_in[i].astype(F32)
    inv = lax.rsqrt(join(total[:, 2 * hid :])[:, :1] / width + EPS)
    gate_pre = total[:, :hid] * inv
    up_pre = total[:, hid : 2 * hid] * inv
    gp_ref[...] = gate_pre
    up_ref[...] = up_pre
    inv_ref[...] = jnp.broadcast_to(inv, (rows, 128))
    act_all[z, :, :hid] = (gate_pre * jax.nn.sigmoid(gate_pre) * up_pre).astype(BF16)
    high, low = split(inv_ref[...])
    act_all[z, :, hid : hid + 128] = high
    act_all[z, :, hid + 128 :] = low
    over_dp("start", mine(act_all), at(act_all), 1)
    loads[4].wait()
    over_dp("wait_recv", mine(act_all), at(act_all), 1)
    act = act_all[...].reshape(slots, hid + 256)
    out_rows = r_slot * jnp.dot(act[:, :hid], wd[...], preferred_element_type=F32)
    cross[s, p] = out_rows.astype(BF16)

    @pl.when(s != nl - 1)
    def _():
        to_section(0, s, cross.at[s, p], lax.rem(s + 1, nl)).start()

    return_rows(0, s, cross[s, p].astype(F32))
    dispatch_wait(1, False)
    g_ref[...] = unpack(1)

    def place_rows(kind, layer, acc):
        return_wait(kind, layer, False)
        want = lax.broadcasted_iota(jnp.int32, (rows, toks), 1).astype(F32) + base
        hot = jnp.where(idsall[layer, me][:, :1] == want, 1.0, 0.0).astype(BF16)
        for q in range(nz):
            got = r_recv[kind, layer, q * ne : (q + 1) * ne].astype(F32)
            got = jnp.concatenate([got[:, :CAP], got[:, CAP:]], axis=-1)
            got = got.reshape(rows, dsl).astype(BF16)
            add = lax.dot_general(hot, got, FIRST, preferred_element_type=F32)
            columns = slice(q * dsl, (q + 1) * dsl)
            acc[:, columns] = (acc[:, columns].astype(F32) + add).astype(BF16)

    store_f = pltpu.make_async_copy(tok, out_f, store_sem.at[0])

    def finish_forward():
        def step(layer, _):
            place_rows(0, layer, tok)
            return 0

        lax.fori_loop(0, s + 1, step, 0)
        store_f.start()

    pl.when(s != nl - 1)(finish_forward)

    def backward_receive(i, _):
        receive(1, nl - 1 - i, g_ref, -1, 0)
        return 0

    lax.fori_loop(0, nl - 1 - s, backward_receive, 0)

    slot_grad = (r_slot * g_ref[...]).astype(BF16)
    hpart[...] = lax.dot_general(
        slot_grad, wd[...], SECOND, preferred_element_type=F32
    ).astype(BF16)
    over_dp("start", block(hpart), at(hpart_in), 2)
    hpart_in[z] = hpart[pl.ds(pl.multiple_of(z * rows, 16), rows)]
    gate_pre = gp_ref[...]
    up_pre = up_ref[...]
    sig = jax.nn.sigmoid(gate_pre)
    over_dp("wait_recv", block(hpart), at(hpart_in), 2)
    hidden = hpart_in[0].astype(F32)
    for i in range(1, nz):
        hidden = hidden + hpart_in[i].astype(F32)
    gate_grad = (hidden * up_pre * sig * (1.0 + gate_pre * (1.0 - sig))).astype(BF16)
    up_grad = (hidden * gate_pre * sig).astype(BF16)
    grad_all[z, :, :hid] = gate_grad
    grad_all[z, :, hid : 2 * hid] = up_grad
    along = jnp.sum(
        gate_grad.astype(F32) * gate_pre + up_grad.astype(F32) * up_pre, axis=1, keepdims=True
    )
    inv = inv_ref[...]
    high, low = split(inv * inv * along / width)
    grad_all[z, :, 2 * hid : 2 * hid + 128] = high
    grad_all[z, :, 2 * hid + 128 :] = low
    over_dp("start", mine(grad_all), at(grad_all), 3)
    over_dp("wait_recv", mine(grad_all), at(grad_all), 3)
    grads = grad_all[...].reshape(slots, 2 * hid + 256)
    act = act_all[...].reshape(slots, hid + 256)
    inv_slot = join(act[:, hid:])[:, :1]
    factor = join(grads[:, 2 * hid :])[:, :1]
    back = lax.dot_general(
        grads[:, :hid], wg[...], SECOND, preferred_element_type=F32
    ) + lax.dot_general(grads[:, hid : 2 * hid], wu[...], SECOND, preferred_element_type=F32)
    own_b[...] = (inv_slot * (gain_row * back) - a_ref[...] * factor).astype(BF16)

    @pl.when(s != 0)
    def _():
        to_section(1, s, own_b, lax.rem(s + nl - 1, nl)).start()

    return_rows(1, s, own_b[...].astype(F32))

    normed = (a_ref[...] * inv_slot * gain_row).astype(BF16)
    step_w = 256 if dsl % 256 == 0 else 128
    stores = []
    for start in range(0, dsl, step_w):
        left = normed[:, start : start + step_w]
        for out, lo in ((wg, 0), (wu, hid)):
            out[start : start + step_w, :] = lax.dot_general(
                left, grads[:, lo : lo + hid], FIRST, preferred_element_type=F32
            ).astype(BF16)
    stores.append(pltpu.make_async_copy(wg, out_g, store_sem.at[2]))
    stores.append(pltpu.make_async_copy(wu, out_u, store_sem.at[3]))
    stores[0].start()
    stores[1].start()
    step_h = 256 if hid % 256 == 0 else 128
    slot_grad = (r_slot * g_ref[...]).astype(BF16)
    for start in range(0, hid, step_h):
        wd[start : start + step_h, :] = lax.dot_general(
            act[:, start : start + step_h], slot_grad, FIRST, preferred_element_type=F32
        ).astype(BF16)
    stores.append(pltpu.make_async_copy(wd, out_d, store_sem.at[4]))
    stores[2].start()

    pl.when(s == nl - 1)(finish_forward)

    def finish_backward(i, _):
        place_rows(1, nl - 1 - i, cot)
        return 0

    lax.fori_loop(0, nl - s, finish_backward, 0)
    store_b = pltpu.make_async_copy(cot, out_b, store_sem.at[1])
    store_b.start()

    dispatch_wait(0, True)
    dispatch_wait(1, True)
    meta("wait_send")
    exchange_ids("wait_send")
    over_dp("wait_send", block(part), at(part_in), 0)
    over_dp("wait_send", mine(act_all), at(act_all), 1)
    over_dp("wait_send", block(hpart), at(hpart_in), 2)
    over_dp("wait_send", mine(grad_all), at(grad_all), 3)

    def drain_forward(layer, _):
        return_wait(0, layer, True)

        @pl.when(s != nl - 1)
        def _():
            to_section(0, layer, cross.at[layer, p], lax.rem(s + 1, nl)).wait_send()

        return 0

    lax.fori_loop(0, s + 1, drain_forward, 0)

    def drain_backward(layer, _):
        return_wait(1, layer, True)

        @pl.when((s != 0) & (layer != s))
        def _():
            to_section(1, layer, cross.at[layer, p], lax.rem(s + nl - 1, nl)).wait_send()

        return 0

    lax.fori_loop(s, nl, drain_backward, 0)

    @pl.when(s != 0)
    def _():
        to_section(1, s, own_b, lax.rem(s + nl - 1, nl)).wait_send()

    def drain_share(layer, _):
        share(layer, "wait_send")
        return 0

    lax.fori_loop(0, s, drain_share, 0)
    lax.fori_loop(s + 1, nl, drain_share, 0)
    for copy in stores:
        copy.wait()
    store_f.wait()
    store_b.wait()


def local(
    tokens, cotangent, norm_gain, route_gates, expert_ids, expert_map, w_gate, w_up, w_down
):
    nz, nl, ne = (lax.axis_size(n) for n in ("dp", "section", "expert"))
    toks, width = tokens.shape
    dsl, hid = w_gate.shape[2:]
    nb = nz * ne
    rows = ne * CAP
    slots = nb * CAP
    half = dsl // 2
    vm = pltpu.VMEM
    dma = pltpu.SemaphoreType.DMA
    anywhere = pl.BlockSpec(memory_space=pl.ANY)
    vmem = pl.BlockSpec(memory_space=pltpu.VMEM)
    smem = pl.BlockSpec(memory_space=pltpu.SMEM)
    out = functools.partial(jax.ShapeDtypeStruct, dtype=BF16)
    results = pl.pallas_call(
        functools.partial(kernel, nz, nl, ne),
        out_shape=(
            out((toks, width)), out((toks, width)), out((dsl, hid)), out((dsl, hid)),
            out((hid, dsl)),
        ),
        in_specs=[anywhere, anywhere, vmem, vmem, vmem, smem, anywhere, anywhere, anywhere],
        out_specs=(anywhere,) * 5,
        scratch_shapes=[
            vm((toks, width), BF16), vm((toks, width), BF16),
            vm((dsl, hid), BF16), vm((dsl, hid), BF16), vm((hid, dsl), BF16),
            vm((2, nb, 2 * CAP, half), BF16), vm((2, nb, 2 * CAP, half), BF16),
            vm((rows, 256), F32), vm((nb, rows, 256), F32),
            vm((nl, nb, rows, 128), F32),
            vm((nl, ne, slots, dsl), BF16), vm((slots, dsl), BF16),
            vm((2, nl, nb, 2 * CAP, half), BF16), vm((2, nl, nb, 2 * CAP, half), BF16),
            vm((slots, dsl), F32), vm((slots, dsl), F32),
            vm((slots, 2 * hid + 256), BF16), vm((nz, rows, 2 * hid + 256), BF16),
            vm((nz, rows, hid + 256), BF16),
            vm((slots, hid), BF16), vm((nz, rows, hid), BF16),
            vm((nz, rows, 2 * hid + 256), BF16),
            vm((rows, hid), F32), vm((rows, hid), F32), vm((rows, 128), F32),
            dma((5,)), dma((5,)),
            dma((2, nb)), dma((2, nb)), dma((nb,)), dma((nb,)),
            dma((nl,)), dma((nl,)), dma((4, nz)), dma((4, nz)),
            dma((2, nl)), dma((2, nl)), dma((nl, ne)), dma((nl, ne)),
            dma((2, nl, nb)), dma((2, nl, nb)),
        ],
        compiler_params=pltpu.CompilerParams(
            collective_id=0, has_side_effects=True, vmem_limit_bytes=58 * 2**20
        ),
    )(
        tokens, cotangent, norm_gain, route_gates[0], expert_ids[0], expert_map,
        w_gate[0, 0], w_up[0, 0], w_down[0, 0],
    )
    layer_out, input_grad, gate, up, down = results
    return layer_out[None], input_grad[None], gate[None, None], up[None, None], down[None, None]


def solution(mesh):
    tokens = P(("dp", "expert"), None)
    routed = P("section", ("dp", "expert"), None)
    wide = P("section", "expert", "dp", None)
    tall = P("section", "expert", None, "dp")
    return jax.shard_map(
        local,
        mesh=mesh,
        in_specs=(
            tokens, tokens, P("section", None), routed, routed, P("section", None),
            wide, wide, tall,
        ),
        out_specs=(routed, routed, wide, wide, tall),
        check_vma=False,
    )
```

```python
import functools

import jax
import jax.numpy as jnp
from jax import lax
from jax.experimental import pallas as pl
from jax.experimental.pallas import tpu as pltpu
from jax.sharding import PartitionSpec as P

CAP = 8
TID = 64
EPS = 1e-06
F32 = jnp.float32
BF16 = jnp.bfloat16
FIRST = (((0,), (0,)), ((), ()))
SECOND = (((1,), (1,)), ((), ()))


def split(value):
    high = value.astype(BF16)
    return high, (value - high.astype(F32)).astype(BF16)


def join(ref_value):
    wide = ref_value.astype(F32)
    return wide[:, :128] + wide[:, 128:]


def kernel(
    nz, nl, ne,
    tok_in, cot_in, gain, gates, ids, emap, wg_in, wu_in, wd_in,
    tok, cot, wg, wu, wd,
    d_send, d_recv, m_send, idsall, cross, own_b, r_send, r_recv,
    a_ref, g_ref, part, part_in, act_all, hpart, hpart_in, grad_all,
    gp_ref, up_ref, inv_ref,
    load_sem, d_ss, d_rs, m_ss, m_rs, i_ss, i_rs, c_ss, c_rs,
    f_ss, f_rs, x_ss, x_rs, r_ss, r_rs,
):
    z, s, p = lax.axis_index("dp"), lax.axis_index("section"), lax.axis_index("expert")
    nb = nz * ne
    me = z * ne + p
    rows = ne * CAP
    slots = nb * CAP
    toks, width = tok.shape
    dsl = width // nz
    half = dsl // 2
    hid = wg.shape[1]

    def rdma(src, dst, ss, rs, zz, sec, ex):
        return pltpu.make_async_remote_copy(
            src_ref=src, dst_ref=dst, send_sem=ss, recv_sem=rs,
            device_id={"dp": zz, "section": sec, "expert": ex},
            device_id_type=pl.DeviceIdType.MESH,
        )

    loads = [
        pltpu.make_async_copy(a, b, load_sem.at[i])
        for i, (a, b) in enumerate(
            ((tok_in, tok), (cot_in, cot), (wg_in, wg), (wu_in, wu), (wd_in, wd))
        )
    ]
    for copy in loads:
        copy.start()

    barrier = pltpu.get_barrier_semaphore()

    def greet(d, _):
        other = lax.rem(me + d, nb)
        pl.semaphore_signal(
            barrier, inc=1,
            device_id={"dp": other // ne, "section": s, "expert": lax.rem(other, ne)},
            device_id_type=pl.DeviceIdType.MESH,
        )
        return 0

    lax.fori_loop(1, nb, greet, 0)

    def greet_section(d, _):
        pl.semaphore_signal(
            barrier, inc=1,
            device_id={"dp": z, "section": lax.rem(s + d, nl), "expert": p},
            device_id_type=pl.DeviceIdType.MESH,
        )
        return 0

    lax.fori_loop(1, nl, greet_section, 0)

    row = lax.broadcasted_iota(jnp.int32, (rows, toks), 0)
    token = lax.broadcasted_iota(jnp.int32, (rows, toks), 1)
    expert = jnp.full((rows, toks), -1, jnp.int32)
    place = row
    for e in range(ne):
        here = (row >= e * CAP) & (row < (e + 1) * CAP)
        expert = jnp.where(here, emap[0, e], expert)
        place = jnp.where(here, row - e * CAP, place)
    chosen = jnp.zeros((rows, toks), F32)
    weight = jnp.zeros((rows, toks), F32)
    for k in range(ids.shape[0]):
        match = ids[k] == expert
        chosen = chosen + jnp.where(match, 1.0, 0.0)
        weight = weight + jnp.where(match, gates[k], 0.0)
    tri_r = lax.broadcasted_iota(jnp.int32, (toks, toks), 0)
    tri_c = lax.broadcasted_iota(jnp.int32, (toks, toks), 1)
    tri = jnp.where(tri_r <= tri_c, 1.0, 0.0).astype(BF16)
    rank = jnp.dot(chosen.astype(BF16), tri, preferred_element_type=F32)
    placed = jnp.where(rank - 1.0 == place.astype(F32), chosen, 0.0)
    r_col = jnp.sum(placed * weight, axis=1, keepdims=True)
    t_col = jnp.sum(placed * (token + 1).astype(F32), axis=1, keepdims=True)
    base = (me * toks).astype(F32)
    t_col = jnp.where(t_col > 0.5, t_col - 1.0 + base, -1.0)
    lane = lax.broadcasted_iota(jnp.int32, (rows, 128), 1)
    m_send[...] = jnp.where(lane < TID, r_col, t_col)
    idsall[s, me] = m_send[...]
    pick = placed.astype(BF16)

    pl.semaphore_wait(barrier, nb - 1 + nl - 1)

    def pack(value):
        return jnp.concatenate([value[..., :half], value[..., half:]], axis=-2)

    def gather(kind, source):
        for q in range(nz):
            got = jnp.dot(
                pick, source[:, q * dsl : (q + 1) * dsl], preferred_element_type=F32
            )
            for e in range(ne):
                d_send[kind, q * ne + e] = pack(got[e * CAP : (e + 1) * CAP]).astype(BF16)
        d_recv[kind, me] = d_send[kind, me]

    def dispatch(kind):
        def send(d, _):
            other = lax.rem(me + d, nb)
            rdma(
                d_send.at[kind, other], d_recv.at[kind, me], d_ss.at[kind, d], d_rs.at[kind, d],
                other // ne, s, lax.rem(other, ne),
            ).start()
            return 0

        lax.fori_loop(1, nb, send, 0)

    def dispatch_wait(kind, sent):
        def wait(d, _):
            other = lax.rem(me + nb - d, nb)
            copy = rdma(
                d_send.at[kind, other], d_recv.at[kind, other], d_ss.at[kind, d],
                d_rs.at[kind, d], other // ne, s, lax.rem(other, ne),
            )
            if sent:
                copy.wait_send()
            else:
                copy.wait_recv()
            return 0

        lax.fori_loop(1, nb, wait, 0)

    def meta(action):
        def step(d, _):
            other = lax.rem(me + d, nb)
            source = lax.rem(me + nb - d, nb)
            where = me if action == "start" else source
            copy = rdma(
                m_send, idsall.at[s, where], m_ss.at[d], m_rs.at[d],
                other // ne, s, lax.rem(other, ne),
            )
            getattr(copy, action)()
            return 0

        lax.fori_loop(1, nb, step, 0)

    def exchange_ids(action):
        def step(d, _):
            other = lax.rem(s + d, nl)
            source = lax.rem(s + nl - d, nl)
            where = s if action == "start" else source
            copy = rdma(idsall.at[s], idsall.at[where], i_ss.at[d], i_rs.at[d], z, other, p)
            getattr(copy, action)()
            return 0

        lax.fori_loop(1, nl, step, 0)

    loads[0].wait()
    gather(0, tok)
    dispatch(0)
    meta("start")

    def meta_settle():
        meta("wait_recv")
        exchange_ids("start")

    def cot_settle():
        loads[1].wait()
        gather(1, cot)
        dispatch(1)

    @pl.when(s != 0)
    def _():
        meta_settle()
        cot_settle()

    own_rows = pl.ds(pl.multiple_of(p * CAP, CAP), CAP)

    def own_meta():
        return idsall[s, :, own_rows, :].reshape(slots, 128)

    gain_row = gain[:, pl.ds(pl.multiple_of(z * dsl, 128), dsl)]

    def unpack(kind):
        value = d_recv[kind].astype(F32)
        return jnp.concatenate([value[:, :CAP], value[:, CAP:]], axis=-1).reshape(slots, dsl)

    dispatch_wait(0, False)
    a_ref[...] = unpack(0)

    def over_dp(action, send_at, recv_at, which):
        def step(d, _):
            other = lax.rem(z + d, nz)
            source = lax.rem(z + nz - d, nz)
            where = z if action == "start" else source
            copy = rdma(
                send_at(other), recv_at(where), c_ss.at[which, d], c_rs.at[which, d],
                other, s, p,
            )
            getattr(copy, action)()
            return 0

        lax.fori_loop(1, nz, step, 0)

    def block(ref):
        return lambda other: ref.at[pl.ds(pl.multiple_of(other * rows, 16), rows)]

    def mine(ref):
        return lambda other: ref.at[z]

    def at(ref):
        return lambda where: ref.at[where]

    def return_rows(kind, layer, source):
        value = source[...].astype(F32).reshape(2, nb, CAP, half)
        r_send[kind, layer] = jnp.concatenate([value[0], value[1]], axis=1).astype(BF16)
        r_recv[kind, layer, me] = r_send[kind, layer, me]

        def send(d, _):
            other = lax.rem(me + d, nb)
            rdma(
                r_send.at[kind, layer, other], r_recv.at[kind, layer, me],
                r_ss.at[kind, layer, d], r_rs.at[kind, layer, d],
                other // ne, s, lax.rem(other, ne),
            ).start()
            return 0

        lax.fori_loop(1, nb, send, 0)

    def return_wait(kind, layer, sent):
        def wait(d, _):
            other = lax.rem(me + nb - d, nb)
            copy = rdma(
                r_send.at[kind, layer, other], r_recv.at[kind, layer, other],
                r_ss.at[kind, layer, d], r_rs.at[kind, layer, d],
                other // ne, s, lax.rem(other, ne),
            )
            if sent:
                copy.wait_send()
            else:
                copy.wait_recv()
            return 0

        lax.fori_loop(1, nb, wait, 0)

    def to_section(kind, layer, src, sec, c):
        return rdma(
            src, cross.at[layer, p, c], f_ss.at[kind, layer, c], f_rs.at[kind, layer, c],
            z, sec, p,
        )

    def share(layer, action, c):
        def step(d, _):
            other = lax.rem(p + d, ne)
            source = lax.rem(p + ne - d, ne)
            where = p if action != "wait_recv" else source
            copy = rdma(
                cross.at[layer, p, c], cross.at[layer, where, c], x_ss.at[layer, d, c],
                x_rs.at[layer, d, c], z, s, other,
            )
            getattr(copy, action)()
            return 0

        lax.fori_loop(1, ne, step, 0)

    def receive(kind, layer, state, step_to, last):
        matches = []
        mine_t = own_meta()[:, TID : TID + 1]
        for e in range(ne):
            theirs = idsall[layer, :, e * CAP : (e + 1) * CAP, :].reshape(slots, 128)
            theirs = jnp.transpose(theirs)[TID : TID + 1]
            matches.append(jnp.where(mine_t == theirs, 1.0, 0.0).astype(BF16))
        further = lax.rem(s + nl + step_to, nl)
        for c in range(2):
            to_section(kind, layer, cross.at[layer, p, c], further, c).wait_recv()
            share(layer, "start", c)

            @pl.when(s != last)
            def _():
                to_section(kind, layer, cross.at[layer, p, c], further, c).start()

        for c in range(2):
            share(layer, "wait_recv", c)
            columns = slice(c * half, (c + 1) * half)
            total = state[:, columns]
            for e in range(ne):
                total = total + jnp.dot(
                    matches[e], cross[layer, e, c], preferred_element_type=F32
                )
            state[:, columns] = total.astype(BF16).astype(F32)

    def part_back():
        slot_grad = (own_meta()[:, 0:1] * g_ref[...]).astype(BF16)
        hpart[...] = lax.dot_general(
            slot_grad, wd[...], SECOND, preferred_element_type=F32
        ).astype(BF16)
        over_dp("start", block(hpart), at(hpart_in), 2)
        hpart_in[z] = hpart[pl.ds(pl.multiple_of(z * rows, 16), rows)]

    @pl.when(s != 0)
    def _():
        exchange_ids("wait_recv")

    @pl.when(s == nl - 1)
    def _():
        dispatch_wait(1, False)
        g_ref[...] = unpack(1)
        loads[4].wait()
        part_back()

    def forward_receive(layer, _):
        receive(0, layer, a_ref, 1, nl - 1)
        return 0

    lax.fori_loop(0, s, forward_receive, 0)

    wide = a_ref[...]
    x = (wide * gain_row).astype(BF16)
    square = jnp.sum(wide * wide, axis=1, keepdims=True)
    loads[2].wait()
    part[:, :hid] = jnp.dot(x, wg[...], preferred_element_type=F32).astype(BF16)
    loads[3].wait()
    part[:, hid : 2 * hid] = jnp.dot(x, wu[...], preferred_element_type=F32).astype(BF16)
    high, low = split(jnp.broadcast_to(square, (slots, 128)))
    part[:, 2 * hid : 2 * hid + 128] = high
    part[:, 2 * hid + 128 :] = low
    over_dp("start", block(part), at(part_in), 0)
    part_in[z] = part[pl.ds(pl.multiple_of(z * rows, 16), rows)]
    pl.when(s == 0)(meta_settle)
    over_dp("wait_recv", block(part), at(part_in), 0)
    total = part_in[0].astype(F32)
    for i in range(1, nz):
        total = total + part_in[i].astype(F32)
    inv = lax.rsqrt(join(total[:, 2 * hid :])[:, :1] / width + EPS)
    gate_pre = total[:, :hid] * inv
    up_pre = total[:, hid : 2 * hid] * inv
    gp_ref[...] = gate_pre
    up_ref[...] = up_pre
    inv_ref[...] = jnp.broadcast_to(inv, (rows, 128))
    act_all[z, :, :hid] = (gate_pre * jax.nn.sigmoid(gate_pre) * up_pre).astype(BF16)
    high, low = split(inv_ref[...])
    act_all[z, :, hid : hid + 128] = high
    act_all[z, :, hid + 128 :] = low
    over_dp("start", mine(act_all), at(act_all), 1)

    @pl.when(s == 0)
    def _():
        cot_settle()

    @pl.when(s != nl - 1)
    def _():
        loads[4].wait()

    r_slot = own_meta()[:, 0:1]
    over_dp("wait_recv", mine(act_all), at(act_all), 1)
    act = act_all[...].reshape(slots, hid + 256)
    for c in range(2):
        out_rows = r_slot * jnp.dot(
            act[:, :hid], wd[:, c * half : (c + 1) * half], preferred_element_type=F32
        )
        cross[s, p, c] = out_rows.astype(BF16)

        @pl.when(s != nl - 1)
        def _():
            to_section(0, s, cross.at[s, p, c], lax.rem(s + 1, nl), c).start()

    def return_forward():
        def step(layer, _):
            return_rows(0, layer, cross.at[layer, p])
            return 0

        lax.fori_loop(0, s + 1, step, 0)

    @pl.when(s != nl - 1)
    def _():
        return_forward()
        dispatch_wait(1, False)
        g_ref[...] = unpack(1)

    @pl.when(s == 0)
    def _():
        exchange_ids("wait_recv")

    def place_rows(kind, layer, acc):
        return_wait(kind, layer, False)
        want = lax.broadcasted_iota(jnp.int32, (rows, toks), 1).astype(F32) + base
        hot = jnp.where(idsall[layer, me][:, TID : TID + 1] == want, 1.0, 0.0).astype(BF16)
        for q in range(nz):
            got = r_recv[kind, layer, q * ne : (q + 1) * ne].astype(F32)
            got = jnp.concatenate([got[:, :CAP], got[:, CAP:]], axis=-1)
            got = got.reshape(rows, dsl).astype(BF16)
            add = lax.dot_general(hot, got, FIRST, preferred_element_type=F32)
            columns = slice(q * dsl, (q + 1) * dsl)
            acc[:, columns] = (acc[:, columns].astype(F32) + add).astype(BF16)

    def finish_forward():
        def step(layer, _):
            place_rows(0, layer, tok)
            return 0

        lax.fori_loop(0, s + 1, step, 0)

    pl.when(s != nl - 1)(finish_forward)

    def backward_receive(i, _):
        receive(1, nl - 1 - i, g_ref, -1, 0)

        @pl.when(nl - 1 - i > s + 1)
        def _():
            return_rows(1, nl - 1 - i, cross.at[nl - 1 - i, p])

        return 0

    lax.fori_loop(0, nl - 1 - s, backward_receive, 0)

    pl.when(s != nl - 1)(part_back)
    gate_pre = gp_ref[...]
    up_pre = up_ref[...]
    sig = jax.nn.sigmoid(gate_pre)
    over_dp("wait_recv", block(hpart), at(hpart_in), 2)
    hidden = hpart_in[0].astype(F32)
    for i in range(1, nz):
        hidden = hidden + hpart_in[i].astype(F32)
    gate_grad = (hidden * up_pre * sig * (1.0 + gate_pre * (1.0 - sig))).astype(BF16)
    up_grad = (hidden * gate_pre * sig).astype(BF16)
    grad_all[z, :, :hid] = gate_grad
    grad_all[z, :, hid : 2 * hid] = up_grad
    along = jnp.sum(
        gate_grad.astype(F32) * gate_pre + up_grad.astype(F32) * up_pre, axis=1, keepdims=True
    )
    inv = inv_ref[...]
    high, low = split(inv * inv * along / width)
    grad_all[z, :, 2 * hid : 2 * hid + 128] = high
    grad_all[z, :, 2 * hid + 128 :] = low
    over_dp("start", mine(grad_all), at(grad_all), 3)

    @pl.when(s != nl - 1)
    def _():
        return_rows(1, s + 1, cross.at[lax.rem(s + 1, nl), p])

    over_dp("wait_recv", mine(grad_all), at(grad_all), 3)
    grads = grad_all[...].reshape(slots, 2 * hid + 256)
    act = act_all[...].reshape(slots, hid + 256)
    inv_slot = join(act[:, hid:])[:, :1]
    factor = join(grads[:, 2 * hid :])[:, :1]
    for c in range(2):
        columns = slice(c * half, (c + 1) * half)
        back = lax.dot_general(
            grads[:, :hid], wg[columns, :], SECOND, preferred_element_type=F32
        ) + lax.dot_general(
            grads[:, hid : 2 * hid], wu[columns, :], SECOND, preferred_element_type=F32
        )
        own_b[c] = (
            inv_slot * (gain_row[:, columns] * back) - a_ref[:, columns] * factor
        ).astype(BF16)

        @pl.when(s != 0)
        def _():
            to_section(1, s, own_b.at[c], lax.rem(s + nl - 1, nl), c).start()

    return_rows(1, s, own_b)
    pl.when(s == nl - 1)(return_forward)

    normed = (a_ref[...] * inv_slot * gain_row).astype(BF16)
    step_w = 256 if dsl % 256 == 0 else 128
    for start in range(0, dsl, step_w):
        left = normed[:, start : start + step_w]
        for out, lo in ((wg, 0), (wu, hid)):
            out[start : start + step_w, :] = lax.dot_general(
                left, grads[:, lo : lo + hid], FIRST, preferred_element_type=F32
            ).astype(BF16)
    step_h = 256 if hid % 256 == 0 else 128
    slot_grad = (r_slot * g_ref[...]).astype(BF16)
    for start in range(0, hid, step_h):
        wd[start : start + step_h, :] = lax.dot_general(
            act[:, start : start + step_h], slot_grad, FIRST, preferred_element_type=F32
        ).astype(BF16)

    pl.when(s == nl - 1)(finish_forward)

    def finish_backward(i, _):
        place_rows(1, nl - 1 - i, cot)
        return 0

    lax.fori_loop(0, nl - s, finish_backward, 0)

    dispatch_wait(0, True)
    dispatch_wait(1, True)
    meta("wait_send")
    exchange_ids("wait_send")
    over_dp("wait_send", block(part), at(part_in), 0)
    over_dp("wait_send", mine(act_all), at(act_all), 1)
    over_dp("wait_send", block(hpart), at(hpart_in), 2)
    over_dp("wait_send", mine(grad_all), at(grad_all), 3)

    def drain_forward(layer, _):
        return_wait(0, layer, True)

        @pl.when(s != nl - 1)
        def _():
            for c in range(2):
                to_section(0, layer, cross.at[layer, p, c], lax.rem(s + 1, nl), c).wait_send()

        return 0

    lax.fori_loop(0, s + 1, drain_forward, 0)

    def drain_backward(layer, _):
        return_wait(1, layer, True)

        @pl.when((s != 0) & (layer != s))
        def _():
            for c in range(2):
                to_section(
                    1, layer, cross.at[layer, p, c], lax.rem(s + nl - 1, nl), c
                ).wait_send()

        return 0

    lax.fori_loop(s, nl, drain_backward, 0)

    @pl.when(s != 0)
    def _():
        for c in range(2):
            to_section(1, s, own_b.at[c], lax.rem(s + nl - 1, nl), c).wait_send()

    def drain_share(layer, _):
        for c in range(2):
            share(layer, "wait_send", c)
        return 0

    lax.fori_loop(0, s, drain_share, 0)
    lax.fori_loop(s + 1, nl, drain_share, 0)


def write_out(*refs):
    count = (len(refs) - 1) // 2
    copies = [
        pltpu.make_async_copy(refs[i], refs[count + i], refs[-1].at[i]) for i in range(count)
    ]
    for copy in copies:
        copy.start()
    for copy in copies:
        copy.wait()


def local(
    tokens, cotangent, norm_gain, route_gates, expert_ids, expert_map, w_gate, w_up, w_down
):
    nz, nl, ne = (lax.axis_size(n) for n in ("dp", "section", "expert"))
    toks, width = tokens.shape
    dsl, hid = w_gate.shape[2:]
    nb = nz * ne
    rows = ne * CAP
    slots = nb * CAP
    half = dsl // 2
    vm = pltpu.VMEM
    dma = pltpu.SemaphoreType.DMA
    anywhere = pl.BlockSpec(memory_space=pl.ANY)
    vmem = pl.BlockSpec(memory_space=pltpu.VMEM)
    smem = pl.BlockSpec(memory_space=pltpu.SMEM)
    out = functools.partial(jax.ShapeDtypeStruct, dtype=BF16)
    results = pl.pallas_call(
        functools.partial(kernel, nz, nl, ne),
        out_shape=(
            vm((toks, width), BF16), vm((toks, width), BF16), vm((dsl, hid), BF16),
            vm((dsl, hid), BF16), vm((hid, dsl), BF16),
        ),
        in_specs=[anywhere, anywhere, vmem, vmem, vmem, smem, anywhere, anywhere, anywhere],
        out_specs=(vmem,) * 5,
        scratch_shapes=[
            vm((2, nb, 2 * CAP, half), BF16), vm((2, nb, 2 * CAP, half), BF16),
            vm((rows, 128), F32),
            vm((nl, nb, rows, 128), F32),
            vm((nl, ne, 2, slots, half), BF16), vm((2, slots, half), BF16),
            vm((2, nl, nb, 2 * CAP, half), BF16), vm((2, nl, nb, 2 * CAP, half), BF16),
            vm((slots, dsl), F32), vm((slots, dsl), F32),
            vm((slots, 2 * hid + 256), BF16), vm((nz, rows, 2 * hid + 256), BF16),
            vm((nz, rows, hid + 256), BF16),
            vm((slots, hid), BF16), vm((nz, rows, hid), BF16),
            vm((nz, rows, 2 * hid + 256), BF16),
            vm((rows, hid), F32), vm((rows, hid), F32), vm((rows, 128), F32),
            dma((5,)),
            dma((2, nb)), dma((2, nb)), dma((nb,)), dma((nb,)),
            dma((nl,)), dma((nl,)), dma((4, nz)), dma((4, nz)),
            dma((2, nl, 2)), dma((2, nl, 2)), dma((nl, ne, 2)), dma((nl, ne, 2)),
            dma((2, nl, nb)), dma((2, nl, nb)),
        ],
        compiler_params=pltpu.CompilerParams(
            collective_id=0, has_side_effects=True, vmem_limit_bytes=50 * 2**20
        ),
    )(
        tokens, cotangent, norm_gain, jnp.transpose(route_gates, (2, 0, 1)),
        jnp.transpose(expert_ids, (2, 0, 1)), expert_map,
        w_gate[0, 0], w_up[0, 0], w_down[0, 0],
    )
    layer_out, input_grad, gate, up, down = pl.pallas_call(
        write_out,
        out_shape=tuple(out(r.shape) for r in results),
        in_specs=[anywhere] * 5,
        out_specs=(anywhere,) * 5,
        scratch_shapes=[dma((5,))],
        compiler_params=pltpu.CompilerParams(vmem_limit_bytes=2**20),
    )(*[pltpu.with_memory_space_constraint(r, pltpu.VMEM) for r in results])
    return layer_out[None], input_grad[None], gate[None, None], up[None, None], down[None, None]


def solution(mesh):
    tokens = P(("dp", "expert"), None)
    routed = P("section", ("dp", "expert"), None)
    wide = P("section", "expert", "dp", None)
    tall = P("section", "expert", None, "dp")
    return jax.shard_map(
        local,
        mesh=mesh,
        in_specs=(
            tokens, tokens, P("section", None), routed, routed, P("section", None),
            wide, wide, tall,
        ),
        out_specs=(routed, routed, wide, wide, tall),
        check_vma=False,
    )
```

```python
import functools

import jax
import jax.numpy as jnp
from jax import lax
from jax.experimental import pallas as pl
from jax.experimental.pallas import tpu as pltpu
from jax.sharding import PartitionSpec as P

CAP = 8
TID = 64
EPS = 1e-06
F32 = jnp.float32
BF16 = jnp.bfloat16
FIRST = (((0,), (0,)), ((), ()))
SECOND = (((1,), (1,)), ((), ()))


def split(value):
    high = value.astype(BF16).astype(F32)
    lane = lax.broadcasted_iota(jnp.int32, (value.shape[0], 128), 1)
    return jnp.where(lane < TID, high, value - high).astype(BF16)


def join(value):
    wide = value.astype(F32)
    return wide[:, :1] + wide[:, TID : TID + 1]


def kernel(
    nz, nl, ne,
    tok_in, cot_in, gain, gates, ids, emap, wg_in, wu_in, wd_in,
    tok, cot, wg, wu, wd,
    d_send, d_recv, m_send, idsall, cross, own_b, r_send, r_recv,
    a_ref, g_ref, back_ref, part, part_in, part_u, part_u_in, act_all, hpart, hpart_in,
    grad_all, grad_u,
    gp_ref, up_ref, inv_ref,
    load_sem, d_ss, d_rs, m_ss, m_rs, i_ss, i_rs, c_ss, c_rs,
    f_ss, f_rs, x_ss, x_rs, r_ss, r_rs,
):
    z, s, p = lax.axis_index("dp"), lax.axis_index("section"), lax.axis_index("expert")
    nb = nz * ne
    me = z * ne + p
    rows = ne * CAP
    slots = nb * CAP
    toks, width = tok.shape
    dsl = width // nz
    half = dsl // 2
    hid = wg.shape[1]

    def rdma(src, dst, ss, rs, zz, sec, ex):
        return pltpu.make_async_remote_copy(
            src_ref=src, dst_ref=dst, send_sem=ss, recv_sem=rs,
            device_id={"dp": zz, "section": sec, "expert": ex},
            device_id_type=pl.DeviceIdType.MESH,
        )

    loads = [
        pltpu.make_async_copy(a, b, load_sem.at[i])
        for i, (a, b) in enumerate(
            ((tok_in, tok), (cot_in, cot), (wg_in, wg), (wu_in, wu), (wd_in, wd))
        )
    ]
    for copy in loads:
        copy.start()

    barrier = pltpu.get_barrier_semaphore()

    def greet(d, _):
        other = lax.rem(me + d, nb)
        pl.semaphore_signal(
            barrier, inc=1,
            device_id={"dp": other // ne, "section": s, "expert": lax.rem(other, ne)},
            device_id_type=pl.DeviceIdType.MESH,
        )
        return 0

    lax.fori_loop(1, nb, greet, 0)

    def greet_section(d, _):
        pl.semaphore_signal(
            barrier, inc=1,
            device_id={"dp": z, "section": lax.rem(s + d, nl), "expert": p},
            device_id_type=pl.DeviceIdType.MESH,
        )
        return 0

    lax.fori_loop(1, nl, greet_section, 0)

    row = lax.broadcasted_iota(jnp.int32, (rows, toks), 0)
    token = lax.broadcasted_iota(jnp.int32, (rows, toks), 1)
    expert = jnp.full((rows, toks), -1, jnp.int32)
    place = row
    for e in range(ne):
        here = (row >= e * CAP) & (row < (e + 1) * CAP)
        expert = jnp.where(here, emap[0, e], expert)
        place = jnp.where(here, row - e * CAP, place)
    chosen = jnp.zeros((rows, toks), F32)
    weight = jnp.zeros((rows, toks), F32)
    for k in range(ids.shape[0]):
        match = ids[k] == expert
        chosen = chosen + jnp.where(match, 1.0, 0.0)
        weight = weight + jnp.where(match, gates[k], 0.0)
    tri_r = lax.broadcasted_iota(jnp.int32, (toks, toks), 0)
    tri_c = lax.broadcasted_iota(jnp.int32, (toks, toks), 1)
    tri = jnp.where(tri_r <= tri_c, 1.0, 0.0).astype(BF16)
    rank = jnp.dot(chosen.astype(BF16), tri, preferred_element_type=F32)
    placed = jnp.where(rank - 1.0 == place.astype(F32), chosen, 0.0)
    r_col = jnp.sum(placed * weight, axis=1, keepdims=True)
    t_col = jnp.sum(placed * (token + 1).astype(F32), axis=1, keepdims=True)
    base = (me * toks).astype(F32)
    t_col = jnp.where(t_col > 0.5, t_col - 1.0 + base, -1.0)
    lane = lax.broadcasted_iota(jnp.int32, (rows, 128), 1)
    m_send[...] = jnp.where(lane < TID, r_col, t_col)
    idsall[s, me] = m_send[...]
    pick = placed.astype(BF16)

    pl.semaphore_wait(barrier, nb - 1 + nl - 1)

    def pack(value):
        return jnp.concatenate([value[..., :half], value[..., half:]], axis=-2)

    def gather(kind, source):
        for q in range(nz):
            got = jnp.dot(
                pick, source[:, q * dsl : (q + 1) * dsl], preferred_element_type=F32
            )
            for e in range(ne):
                d_send[kind, q * ne + e] = pack(got[e * CAP : (e + 1) * CAP]).astype(BF16)
        d_recv[kind, me] = d_send[kind, me]

    def dispatch(kind):
        def send(d, _):
            other = lax.rem(me + d, nb)
            rdma(
                d_send.at[kind, other], d_recv.at[kind, me], d_ss.at[kind, d], d_rs.at[kind, d],
                other // ne, s, lax.rem(other, ne),
            ).start()
            return 0

        lax.fori_loop(1, nb, send, 0)

    def dispatch_wait(kind, sent):
        def wait(d, _):
            other = lax.rem(me + nb - d, nb)
            copy = rdma(
                d_send.at[kind, other], d_recv.at[kind, other], d_ss.at[kind, d],
                d_rs.at[kind, d], other // ne, s, lax.rem(other, ne),
            )
            if sent:
                copy.wait_send()
            else:
                copy.wait_recv()
            return 0

        lax.fori_loop(1, nb, wait, 0)

    def meta(action):
        def step(d, _):
            other = lax.rem(me + d, nb)
            source = lax.rem(me + nb - d, nb)
            where = me if action == "start" else source
            copy = rdma(
                m_send, idsall.at[s, where], m_ss.at[d], m_rs.at[d],
                other // ne, s, lax.rem(other, ne),
            )
            getattr(copy, action)()
            return 0

        lax.fori_loop(1, nb, step, 0)

    def exchange_ids(action):
        def step(d, _):
            other = lax.rem(s + d, nl)
            source = lax.rem(s + nl - d, nl)
            where = s if action == "start" else source
            copy = rdma(idsall.at[s], idsall.at[where], i_ss.at[d], i_rs.at[d], z, other, p)
            getattr(copy, action)()
            return 0

        lax.fori_loop(1, nl, step, 0)

    loads[0].wait()
    gather(0, tok)
    dispatch(0)
    meta("start")

    def meta_settle():
        meta("wait_recv")
        exchange_ids("start")

    def cot_settle():
        loads[1].wait()
        gather(1, cot)
        dispatch(1)

    @pl.when(s != 0)
    def _():
        meta_settle()
        cot_settle()

    own_rows = pl.ds(pl.multiple_of(p * CAP, CAP), CAP)

    def own_meta():
        return idsall[s, :, own_rows, :].reshape(slots, 128)

    gain_row = gain[:, pl.ds(pl.multiple_of(z * dsl, 128), dsl)]

    def unpack(kind):
        value = d_recv[kind].astype(F32)
        return jnp.concatenate([value[:, :CAP], value[:, CAP:]], axis=-1).reshape(slots, dsl)

    dispatch_wait(0, False)
    a_ref[...] = unpack(0)

    def over_dp(action, send_at, recv_at, which):
        def step(d, _):
            other = lax.rem(z + d, nz)
            source = lax.rem(z + nz - d, nz)
            where = z if action == "start" else source
            copy = rdma(
                send_at(other), recv_at(where), c_ss.at[which, d], c_rs.at[which, d],
                other, s, p,
            )
            getattr(copy, action)()
            return 0

        lax.fori_loop(1, nz, step, 0)

    def block(ref):
        return lambda other: ref.at[pl.ds(pl.multiple_of(other * rows, 16), rows)]

    def mine(ref):
        return lambda other: ref.at[z]

    def at(ref):
        return lambda where: ref.at[where]

    def return_rows(kind, layer, source):
        value = source[...].astype(F32).reshape(2, nb, CAP, half)
        r_send[kind, layer] = jnp.concatenate([value[0], value[1]], axis=1).astype(BF16)
        r_recv[kind, layer, me] = r_send[kind, layer, me]

        def send(d, _):
            other = lax.rem(me + d, nb)
            rdma(
                r_send.at[kind, layer, other], r_recv.at[kind, layer, me],
                r_ss.at[kind, layer, d], r_rs.at[kind, layer, d],
                other // ne, s, lax.rem(other, ne),
            ).start()
            return 0

        lax.fori_loop(1, nb, send, 0)

    def return_wait(kind, layer, sent):
        def wait(d, _):
            other = lax.rem(me + nb - d, nb)
            copy = rdma(
                r_send.at[kind, layer, other], r_recv.at[kind, layer, other],
                r_ss.at[kind, layer, d], r_rs.at[kind, layer, d],
                other // ne, s, lax.rem(other, ne),
            )
            if sent:
                copy.wait_send()
            else:
                copy.wait_recv()
            return 0

        lax.fori_loop(1, nb, wait, 0)

    def to_section(kind, layer, src, sec, c):
        return rdma(
            src, cross.at[layer, p, c], f_ss.at[kind, layer, c], f_rs.at[kind, layer, c],
            z, sec, p,
        )

    def share(layer, action, c):
        def step(d, _):
            other = lax.rem(p + d, ne)
            source = lax.rem(p + ne - d, ne)
            where = p if action != "wait_recv" else source
            copy = rdma(
                cross.at[layer, p, c], cross.at[layer, where, c], x_ss.at[layer, d, c],
                x_rs.at[layer, d, c], z, s, other,
            )
            getattr(copy, action)()
            return 0

        lax.fori_loop(1, ne, step, 0)

    def receive(kind, layer, state, step_to, last):
        matches = []
        mine_t = own_meta()[:, TID : TID + 1]
        for e in range(ne):
            theirs = idsall[layer, :, e * CAP : (e + 1) * CAP, :].reshape(slots, 128)
            theirs = jnp.transpose(theirs)[TID : TID + 1]
            matches.append(jnp.where(mine_t == theirs, 1.0, 0.0).astype(BF16))
        further = lax.rem(s + nl + step_to, nl)
        for c in range(2):
            to_section(kind, layer, cross.at[layer, p, c], further, c).wait_recv()
            share(layer, "start", c)

            @pl.when(s != last)
            def _():
                to_section(kind, layer, cross.at[layer, p, c], further, c).start()

        for c in range(2):
            share(layer, "wait_recv", c)
            columns = slice(c * half, (c + 1) * half)
            total = state[:, columns]
            for e in range(ne):
                total = total + jnp.dot(
                    matches[e], cross[layer, e, c], preferred_element_type=F32
                )
            state[:, columns] = total.astype(BF16).astype(F32)

    def part_back():
        slot_grad = (own_meta()[:, 0:1] * g_ref[...]).astype(BF16)
        hpart[...] = lax.dot_general(
            slot_grad, wd[...], SECOND, preferred_element_type=F32
        ).astype(BF16)
        over_dp("start", block(hpart), at(hpart_in), 2)
        hpart_in[z] = hpart[pl.ds(pl.multiple_of(z * rows, 16), rows)]

    @pl.when(s != 0)
    def _():
        exchange_ids("wait_recv")

    @pl.when(s == nl - 1)
    def _():
        dispatch_wait(1, False)
        g_ref[...] = unpack(1)
        loads[4].wait()
        part_back()

    def forward_receive(layer, _):
        receive(0, layer, a_ref, 1, nl - 1)
        return 0

    lax.fori_loop(0, s, forward_receive, 0)

    wide = a_ref[...]
    x = (wide * gain_row).astype(BF16)
    square = jnp.sum(wide * wide, axis=1, keepdims=True)
    loads[2].wait()
    part[:, :hid] = jnp.dot(x, wg[...], preferred_element_type=F32).astype(BF16)
    part[:, hid:] = split(square)
    over_dp("start", block(part), at(part_in), 0)
    loads[3].wait()
    part_u[...] = jnp.dot(x, wu[...], preferred_element_type=F32).astype(BF16)
    over_dp("start", block(part_u), at(part_u_in), 4)
    part_in[z] = part[pl.ds(pl.multiple_of(z * rows, 16), rows)]
    part_u_in[z] = part_u[pl.ds(pl.multiple_of(z * rows, 16), rows)]
    pl.when(s == 0)(meta_settle)
    over_dp("wait_recv", block(part), at(part_in), 0)
    total = part_in[0].astype(F32)
    for i in range(1, nz):
        total = total + part_in[i].astype(F32)
    inv = lax.rsqrt(join(total[:, hid:]) / width + EPS)
    gate_pre = total[:, :hid] * inv
    scaled = gate_pre * jax.nn.sigmoid(gate_pre)
    over_dp("wait_recv", block(part_u), at(part_u_in), 4)
    total = part_u_in[0].astype(F32)
    for i in range(1, nz):
        total = total + part_u_in[i].astype(F32)
    up_pre = total * inv
    act_all[z, :, :hid] = (scaled * up_pre).astype(BF16)
    act_all[z, :, hid:] = split(inv)
    over_dp("start", mine(act_all), at(act_all), 1)
    gp_ref[...] = gate_pre
    up_ref[...] = up_pre
    inv_ref[...] = jnp.broadcast_to(inv, (rows, 128))

    @pl.when(s != nl - 1)
    def _():
        loads[4].wait()

    r_slot = own_meta()[:, 0:1]
    over_dp("wait_recv", mine(act_all), at(act_all), 1)
    act = act_all[...].reshape(slots, hid + 128)
    for c in range(2):
        out_rows = r_slot * jnp.dot(
            act[:, :hid], wd[:, c * half : (c + 1) * half], preferred_element_type=F32
        )
        cross[s, p, c] = out_rows.astype(BF16)

        @pl.when(s != nl - 1)
        def _():
            to_section(0, s, cross.at[s, p, c], lax.rem(s + 1, nl), c).start()

    def return_forward():
        def step(layer, _):
            return_rows(0, layer, cross.at[layer, p])
            return 0

        lax.fori_loop(0, s + 1, step, 0)

    @pl.when(s != nl - 1)
    def _():
        pl.when(s == 0)(cot_settle)
        return_forward()
        dispatch_wait(1, False)
        g_ref[...] = unpack(1)

    @pl.when(s == 0)
    def _():
        exchange_ids("wait_recv")

    def place_rows(kind, layer, acc):
        return_wait(kind, layer, False)
        want = lax.broadcasted_iota(jnp.int32, (rows, toks), 1).astype(F32) + base
        hot = jnp.where(idsall[layer, me][:, TID : TID + 1] == want, 1.0, 0.0).astype(BF16)
        for q in range(nz):
            got = r_recv[kind, layer, q * ne : (q + 1) * ne].astype(F32)
            got = jnp.concatenate([got[:, :CAP], got[:, CAP:]], axis=-1)
            got = got.reshape(rows, dsl).astype(BF16)
            add = lax.dot_general(hot, got, FIRST, preferred_element_type=F32)
            columns = slice(q * dsl, (q + 1) * dsl)
            acc[:, columns] = (acc[:, columns].astype(F32) + add).astype(BF16)

    def finish_forward():
        def step(layer, _):
            place_rows(0, layer, tok)
            return 0

        lax.fori_loop(0, s + 1, step, 0)

    pl.when(s != nl - 1)(finish_forward)

    def backward_receive(i, _):
        receive(1, nl - 1 - i, g_ref, -1, 0)

        @pl.when(nl - 1 - i > s + 1)
        def _():
            return_rows(1, nl - 1 - i, cross.at[nl - 1 - i, p])

        return 0

    lax.fori_loop(0, nl - 1 - s, backward_receive, 0)

    pl.when(s != nl - 1)(part_back)
    gate_pre = gp_ref[...]
    up_pre = up_ref[...]
    sig = jax.nn.sigmoid(gate_pre)
    over_dp("wait_recv", block(hpart), at(hpart_in), 2)
    hidden = hpart_in[0].astype(F32)
    for i in range(1, nz):
        hidden = hidden + hpart_in[i].astype(F32)
    gate_grad = (hidden * up_pre * sig * (1.0 + gate_pre * (1.0 - sig))).astype(BF16)
    up_grad = (hidden * gate_pre * sig).astype(BF16)
    along = jnp.sum(
        gate_grad.astype(F32) * gate_pre + up_grad.astype(F32) * up_pre, axis=1, keepdims=True
    )
    inv = inv_ref[:, :1]
    grad_all[z, :, :hid] = gate_grad
    grad_all[z, :, hid:] = split(inv * inv * along / width)
    over_dp("start", mine(grad_all), at(grad_all), 3)
    grad_u[z] = up_grad
    over_dp("start", mine(grad_u), at(grad_u), 5)
    act = act_all[...].reshape(slots, hid + 128)
    inv_slot = join(act[:, hid:])
    over_dp("wait_recv", mine(grad_all), at(grad_all), 3)
    grads = grad_all[...].reshape(slots, hid + 128)
    factor = join(grads[:, hid:])
    for c in range(2):
        columns = slice(c * half, (c + 1) * half)
        back_ref[:, columns] = lax.dot_general(
            grads[:, :hid], wg[columns, :], SECOND, preferred_element_type=F32
        )
    over_dp("wait_recv", mine(grad_u), at(grad_u), 5)
    grads_u = grad_u[...].reshape(slots, hid)

    def return_next():
        return_rows(1, s + 1, cross.at[lax.rem(s + 1, nl), p])

    pl.when(s == 0)(return_next)
    for c in range(2):
        columns = slice(c * half, (c + 1) * half)
        back = back_ref[:, columns] + lax.dot_general(
            grads_u, wu[columns, :], SECOND, preferred_element_type=F32
        )
        own_b[c] = (
            inv_slot * (gain_row[:, columns] * back) - a_ref[:, columns] * factor
        ).astype(BF16)

        @pl.when(s != 0)
        def _():
            to_section(1, s, own_b.at[c], lax.rem(s + nl - 1, nl), c).start()

    pl.when((s != 0) & (s != nl - 1))(return_next)
    return_rows(1, s, own_b)
    pl.when(s == nl - 1)(return_forward)

    normed = (a_ref[...] * inv_slot * gain_row).astype(BF16)
    step_w = 256 if dsl % 256 == 0 else 128
    for start in range(0, dsl, step_w):
        left = normed[:, start : start + step_w]
        for out, right in ((wg, grads[:, :hid]), (wu, grads_u)):
            out[start : start + step_w, :] = lax.dot_general(
                left, right, FIRST, preferred_element_type=F32
            ).astype(BF16)
    step_h = 256 if hid % 256 == 0 else 128
    slot_grad = (r_slot * g_ref[...]).astype(BF16)
    for start in range(0, hid, step_h):
        wd[start : start + step_h, :] = lax.dot_general(
            act[:, start : start + step_h], slot_grad, FIRST, preferred_element_type=F32
        ).astype(BF16)

    pl.when(s == nl - 1)(finish_forward)

    def finish_backward(i, _):
        place_rows(1, nl - 1 - i, cot)
        return 0

    lax.fori_loop(0, nl - s, finish_backward, 0)

    dispatch_wait(0, True)
    dispatch_wait(1, True)
    meta("wait_send")
    exchange_ids("wait_send")
    over_dp("wait_send", block(part), at(part_in), 0)
    over_dp("wait_send", mine(act_all), at(act_all), 1)
    over_dp("wait_send", block(hpart), at(hpart_in), 2)
    over_dp("wait_send", mine(grad_all), at(grad_all), 3)
    over_dp("wait_send", block(part_u), at(part_u_in), 4)
    over_dp("wait_send", mine(grad_u), at(grad_u), 5)

    def drain_forward(layer, _):
        return_wait(0, layer, True)

        @pl.when(s != nl - 1)
        def _():
            for c in range(2):
                to_section(0, layer, cross.at[layer, p, c], lax.rem(s + 1, nl), c).wait_send()

        return 0

    lax.fori_loop(0, s + 1, drain_forward, 0)

    def drain_backward(layer, _):
        return_wait(1, layer, True)

        @pl.when((s != 0) & (layer != s))
        def _():
            for c in range(2):
                to_section(
                    1, layer, cross.at[layer, p, c], lax.rem(s + nl - 1, nl), c
                ).wait_send()

        return 0

    lax.fori_loop(s, nl, drain_backward, 0)

    @pl.when(s != 0)
    def _():
        for c in range(2):
            to_section(1, s, own_b.at[c], lax.rem(s + nl - 1, nl), c).wait_send()

    def drain_share(layer, _):
        for c in range(2):
            share(layer, "wait_send", c)
        return 0

    lax.fori_loop(0, s, drain_share, 0)
    lax.fori_loop(s + 1, nl, drain_share, 0)


def write_out(*refs):
    count = (len(refs) - 1) // 2
    copies = [
        pltpu.make_async_copy(refs[i], refs[count + i], refs[-1].at[i]) for i in range(count)
    ]
    for copy in copies:
        copy.start()
    for copy in copies:
        copy.wait()


def local(
    tokens, cotangent, norm_gain, route_gates, expert_ids, expert_map, w_gate, w_up, w_down
):
    nz, nl, ne = (lax.axis_size(n) for n in ("dp", "section", "expert"))
    toks, width = tokens.shape
    dsl, hid = w_gate.shape[2:]
    nb = nz * ne
    rows = ne * CAP
    slots = nb * CAP
    half = dsl // 2
    vm = pltpu.VMEM
    dma = pltpu.SemaphoreType.DMA
    anywhere = pl.BlockSpec(memory_space=pl.ANY)
    vmem = pl.BlockSpec(memory_space=pltpu.VMEM)
    smem = pl.BlockSpec(memory_space=pltpu.SMEM)
    out = functools.partial(jax.ShapeDtypeStruct, dtype=BF16)
    results = pl.pallas_call(
        functools.partial(kernel, nz, nl, ne),
        out_shape=(
            vm((toks, width), BF16), vm((toks, width), BF16), vm((dsl, hid), BF16),
            vm((dsl, hid), BF16), vm((hid, dsl), BF16),
        ),
        in_specs=[anywhere, anywhere, vmem, vmem, vmem, smem, anywhere, anywhere, anywhere],
        out_specs=(vmem,) * 5,
        scratch_shapes=[
            vm((2, nb, 2 * CAP, half), BF16), vm((2, nb, 2 * CAP, half), BF16),
            vm((rows, 128), F32),
            vm((nl, nb, rows, 128), F32),
            vm((nl, ne, 2, slots, half), BF16), vm((2, slots, half), BF16),
            vm((2, nl, nb, 2 * CAP, half), BF16), vm((2, nl, nb, 2 * CAP, half), BF16),
            vm((slots, dsl), F32), vm((slots, dsl), F32), vm((slots, dsl), F32),
            vm((slots, hid + 128), BF16), vm((nz, rows, hid + 128), BF16),
            vm((slots, hid), BF16), vm((nz, rows, hid), BF16),
            vm((nz, rows, hid + 128), BF16),
            vm((slots, hid), BF16), vm((nz, rows, hid), BF16),
            vm((nz, rows, hid + 128), BF16), vm((nz, rows, hid), BF16),
            vm((rows, hid), F32), vm((rows, hid), F32), vm((rows, 128), F32),
            dma((5,)),
            dma((2, nb)), dma((2, nb)), dma((nb,)), dma((nb,)),
            dma((nl,)), dma((nl,)), dma((6, nz)), dma((6, nz)),
            dma((2, nl, 2)), dma((2, nl, 2)), dma((nl, ne, 2)), dma((nl, ne, 2)),
            dma((2, nl, nb)), dma((2, nl, nb)),
        ],
        compiler_params=pltpu.CompilerParams(
            collective_id=0, has_side_effects=True, vmem_limit_bytes=50 * 2**20
        ),
    )(
        tokens, cotangent, norm_gain, jnp.transpose(route_gates, (2, 0, 1)),
        jnp.transpose(expert_ids, (2, 0, 1)), expert_map,
        w_gate[0, 0], w_up[0, 0], w_down[0, 0],
    )
    layer_out, input_grad, gate, up, down = pl.pallas_call(
        write_out,
        out_shape=tuple(out(r.shape) for r in results),
        in_specs=[anywhere] * 5,
        out_specs=(anywhere,) * 5,
        scratch_shapes=[dma((5,))],
        compiler_params=pltpu.CompilerParams(vmem_limit_bytes=2**20),
    )(*[pltpu.with_memory_space_constraint(r, pltpu.VMEM) for r in results])
    return layer_out[None], input_grad[None], gate[None, None], up[None, None], down[None, None]


def solution(mesh):
    tokens = P(("dp", "expert"), None)
    routed = P("section", ("dp", "expert"), None)
    wide = P("section", "expert", "dp", None)
    tall = P("section", "expert", None, "dp")
    return jax.shard_map(
        local,
        mesh=mesh,
        in_specs=(
            tokens, tokens, P("section", None), routed, routed, P("section", None),
            wide, wide, tall,
        ),
        out_specs=(routed, routed, wide, wide, tall),
        check_vma=False,
    )
```
